32 devices in a mesh: ang: 8 (over y, x, core), rad: 4 (over z).
Axes of the slice: x: 2, y: 2, z: 4, core: 2. Of those that a mesh axis runs over, the one named last changes fastest.
Arguments:
- coarse: float32 [1, 8, 32, 512], P(None, 'ang', None, 'rad'), may hold values from -6 to 6
- excite: float32 [1, 16, 64, 1024], P(None, 'ang', None, 'rad'), may hold values from -6 to 6
- kernels: float32 [27, 8, 512], replicated, may hold values from -0.875 to 0.875
- mixing: float32 [8, 8, 512], replicated, may hold values from -1.5 to 1.5
- star_bin: int32 [16, 64, 16], P('ang'), may hold values from 0 to 1023
- star_count: int32 [16, 64], P('ang'), may hold values from 1 to 16
- star_obs: float32 [16, 64, 16], P('ang'), may hold values from 0 to 3
- star_isig: float32 [16, 64, 16], P('ang'), may hold values from 1 to 10
Outputs:
- grad_excite: float32 [1, 16, 64, 1024], P(None, 'ang', None, 'rad')
- grad_coarse: float32 [1, 8, 32, 512], P(None, 'ang', None, 'rad')
The draws below stay inside these ranges and needn't reach their ends.
All inputs are finite; a program needn't handle non-finite values.
Results may differ from the reference program's by a relative error of at most 0.0003.
Values sent between devices are 32-bit elements; how exact they have to be, the bound alone decides.
A program may use at most 64 MiB of HBM per device.

```python
import math
import jax
import jax.numpy as jnp
from jax import lax

S = 1
CB = 32
MSTAR = 16
NAC = 8
NRC = 512
NA = 16
NB = 64
NR = 1024


def plant(values, key, low, top_value):
    longest = values.shape.index(max(values.shape))
    spots = []
    for shift in (0, 1):
        where = [jax.random.randint(jax.random.fold_in(key, axis), (), 0, length) for axis, length in enumerate(values.shape)]
        where[longest] = (where[longest] + shift) % values.shape[longest]
        spots.append(tuple(where))
    return values.at[spots[0]].set(low).at[spots[1]].set(top_value)


def block_levels(stream_key, shape, shards, smallest, top_value):
    loudness, own = 1.0, jax.random.fold_in(stream_key, 6)
    for position, blocks in shards:
        steps = jnp.exp(jax.random.uniform(jax.random.fold_in(own, position), (blocks,), jnp.float32, smallest / len(shards), top_value / len(shards)))
        loudness = loudness * jnp.repeat(steps, shape[position] // blocks).reshape([-1 if axis == position else 1 for axis in range(len(shape))])
    return loudness


def gaussian(key, shape, spread, limit, shards=(), kind=jnp.bfloat16):
    drawn = spread * jax.random.normal(key, shape, jnp.float32)
    if shards:
        drawn = drawn * block_levels(key, shape, shards, -0.22, 0.18)
    return jnp.clip(drawn, -limit, limit).astype(kind)


def setup_inputs(seed: int = 0) -> dict:
    streams_of = jax.random.split(jax.random.key(seed), 9)
    coarse = gaussian(streams_of[0], (S, NAC, CB, NRC), 1.0, 6.0, ((1, 8), (3, 4)), jnp.float32)
    excite = gaussian(streams_of[1], (S, NA, NB, NR), 1.0, 6.0, ((1, 8), (3, 4)), jnp.float32)
    kernels = gaussian(streams_of[2], (27, 8, NRC), 54 ** -0.5, 0.875, (), jnp.float32)
    mixing = gaussian(streams_of[3], (8, 8, NRC), 16 ** -0.5, 1.5, (), jnp.float32)
    star_bin = plant(jax.random.randint(streams_of[4], (NA, NB, MSTAR), 0, NR), jax.random.fold_in(streams_of[4], 1), 0, NR - 1).astype(jnp.int32)
    star_count = plant(jax.random.randint(streams_of[5], (NA, NB), 1, MSTAR + 1), jax.random.fold_in(streams_of[5], 1), 1, MSTAR).astype(jnp.int32)
    star_obs = jnp.clip(3.0 * jax.random.uniform(streams_of[6], (NA, NB, MSTAR), jnp.float32) ** block_levels(streams_of[6], (NA, NB, MSTAR), ((0, 8),), -0.2, 0.2), 0.0, 3.0)
    star_isig = jnp.clip(jnp.exp(math.log(10.0) - 2.3025851 * jax.random.uniform(streams_of[7], (NA, NB, MSTAR), jnp.float32) ** block_levels(streams_of[7], (NA, NB, MSTAR), ((0, 8),), -0.2, 0.2)), 1.0, 10.0)
    return {"coarse": coarse, "excite": excite, "kernels": kernels, "mixing": mixing, "star_bin": star_bin, "star_count": star_count, "star_obs": star_obs, "star_isig": star_isig}


def to_blocks(field):
    na, nb, nr = field.shape
    return field.reshape(na // 2, 2, nb // 2, 2, nr // 2, 2).transpose(1, 3, 5, 0, 2, 4).reshape(8, na // 2, nb // 2, nr // 2)


def from_blocks(blocks):
    _, na, nb, nr = blocks.shape
    return blocks.reshape(2, 2, 2, na, nb, nr).transpose(3, 0, 4, 1, 5, 2).reshape(2 * na, 2 * nb, 2 * nr)


def one_sample(coarse, excite, kernels, mixing, star_bin, star_count, star_obs, star_isig):
    na, nb, nr = coarse.shape
    padded = jnp.pad(coarse, 1)
    fine = jnp.zeros((8, na, nb, nr), jnp.float32)
    for offset in range(27):
        step_a, step_b, step_r = offset // 9, (offset // 3) % 3, offset % 3
        window = padded[step_a:step_a + na, step_b:step_b + nb, step_r:step_r + nr]
        fine = fine + kernels[offset][:, None, None, :] * window[None]
    excite_blocks = to_blocks(excite)
    fine = fine + jnp.einsum("qpr,pabr->qabr", mixing, excite_blocks, precision=lax.Precision.HIGHEST)
    dens = jnp.exp(from_blocks(fine))
    step_len = 1.0 / NR
    extinction = step_len * jnp.cumsum(dens, axis=2)
    pred = jnp.take_along_axis(extinction, star_bin, axis=2)
    live = jnp.arange(MSTAR)[None, None, :] < star_count[:, :, None]
    res = jnp.where(live, (pred - star_obs) * star_isig, 0.0)
    terms = res * star_isig
    rows_a = jnp.broadcast_to(jnp.arange(NA)[:, None, None], star_bin.shape)
    rows_b = jnp.broadcast_to(jnp.arange(NB)[None, :, None], star_bin.shape)
    hits = jnp.zeros((NA, NB, NR), jnp.float32).at[rows_a, rows_b, star_bin].add(terms)
    suffix = jnp.flip(jnp.cumsum(jnp.flip(hits, 2), axis=2), 2)
    grad_fine = to_blocks(dens * step_len * suffix)
    grad_excite = from_blocks(jnp.einsum("qpr,qabr->pabr", mixing, grad_fine, precision=lax.Precision.HIGHEST) + excite_blocks)
    summed = jnp.zeros((na + 2, nb + 2, nr + 2), jnp.float32)
    for offset in range(27):
        step_a, step_b, step_r = offset // 9, (offset // 3) % 3, offset % 3
        contrib = jnp.sum(kernels[offset][:, None, None, :] * grad_fine, axis=0)
        summed = summed.at[step_a:step_a + na, step_b:step_b + nb, step_r:step_r + nr].add(contrib)
    return grad_excite, summed[1:-1, 1:-1, 1:-1]


def reference(coarse, excite, kernels, mixing, star_bin, star_count, star_obs, star_isig):
    def single(pair):
        return one_sample(pair[0], pair[1], kernels, mixing, star_bin, star_count, star_obs, star_isig)

    grad_excite, grad_coarse = lax.map(single, (coarse, excite))
    return grad_excite, grad_coarse
```

```python
import functools

import jax
import jax.numpy as jnp
from jax import lax
from jax.experimental import pallas as pl
from jax.experimental.pallas import tpu as pltpu
from jax.sharding import PartitionSpec as P

MESH = pl.DeviceIdType.MESH
AROUND = [(du, dz) for du in (-1, 0, 1) for dz in (-1, 0, 1) if (du, dz) != (0, 0)]
PAD = 8


def kernel(
    n_ang,
    n_rad,
    coarse_hbm,
    excite_hbm,
    weights_hbm,
    mixing_hbm,
    bin_hbm,
    count_hbm,
    obs_hbm,
    isig_hbm,
    grad_excite_hbm,
    grad_coarse_hbm,
    coarse,
    excite,
    weights,
    mixing,
    bins,
    count,
    obs,
    isig,
    edge_out,
    halo_rows,
    halo_edges,
    windows,
    blocks,
    dens,
    mine,
    parts,
    slopes,
    back_rows_out,
    back_edges_out,
    back_rows,
    back_edges,
    out_excite,
    out_coarse,
    load_sem,
    halo_send,
    halo_recv,
    part_send,
    part_recv,
    back_send,
    back_recv,
    store_sem,
):
    ang = lax.axis_index("ang")
    rad = lax.axis_index("rad")
    cols, depth = coarse.shape
    slots = mine.shape[0]
    half = depth // 2
    step_len = 1.0 / (2 * depth * n_rad)
    f32 = jnp.float32

    def exists(du, dz):
        there = None
        for shift, place, size in ((du, ang, n_ang), (dz, rad, n_rad)):
            if shift == 0:
                continue
            ok = place > 0 if shift < 0 else place < size - 1
            there = ok if there is None else jnp.logical_and(there, ok)
        return there

    def at(du, dz):
        return {"ang": ang + du, "rad": rad + dz}

    def peer(k):
        return {"ang": ang, "rad": lax.rem(rad + k, n_rad)}

    here = pl.ds(pl.multiple_of(rad * depth, depth), depth)
    pairs = [
        (coarse_hbm, coarse),
        (excite_hbm.at[:, :, pl.ds(0, depth)], excite.at[0]),
        (excite_hbm.at[:, :, pl.ds(depth, depth)], excite.at[1]),
        (mixing_hbm.at[:, :, here], mixing),
        (weights_hbm.at[:, :, here], weights),
        (bin_hbm, bins),
        (count_hbm, count),
        (obs_hbm, obs),
        (isig_hbm, isig),
    ]
    loads = [
        pltpu.make_async_copy(source, target, load_sem.at[n])
        for n, (source, target) in enumerate(pairs)
    ]
    for load in loads:
        load.start()

    barrier = pltpu.get_barrier_semaphore()
    beside = [(du, dz) for du, dz in AROUND if du != 0]
    for du, dz in beside:

        @pl.when(exists(du, dz))
        def _():
            pl.semaphore_signal(barrier, inc=1, device_id=at(du, dz), device_id_type=MESH)

    for k in range(1, n_rad):
        pl.semaphore_signal(barrier, inc=1, device_id=peer(k), device_id_type=MESH)

    rows_of = lambda du: 0 if du < 0 else 1
    halo_copies, back_copies = [], []
    for n, (du, dz) in enumerate(AROUND):
        if dz == 0:
            source, target = coarse, halo_rows.at[rows_of(-du)]
            back_source, back_target = back_rows_out.at[rows_of(du)], back_rows.at[rows_of(-du)]
        else:
            source, target = edge_out.at[rows_of(dz)], halo_edges.at[rows_of(-dz), 1 - du]
            back_source = back_edges_out.at[rows_of(dz), 1 + du]
            back_target = back_edges.at[rows_of(-dz), 1 - du]
        halo_copies.append(
            pltpu.make_async_remote_copy(
                src_ref=source, dst_ref=target, send_sem=halo_send.at[n],
                recv_sem=halo_recv.at[n], device_id=at(du, dz), device_id_type=MESH,
            )
        )
        back_copies.append(
            pltpu.make_async_remote_copy(
                src_ref=back_source, dst_ref=back_target, send_sem=back_send.at[n],
                recv_sem=back_recv.at[n], device_id=at(du, dz), device_id_type=MESH,
            )
        )

        @pl.when(jnp.logical_not(exists(-du, -dz)))
        def _():
            target[...] = jnp.zeros(target.shape, f32)
            back_target[...] = jnp.zeros(back_target.shape, f32)

    lane = lax.broadcasted_iota(jnp.int32, (cols, depth), 1)
    row = lax.broadcasted_iota(jnp.int32, (cols, depth), 0)
    diagonal = lane == row

    def pack(column):
        return jnp.sum(jnp.where(diagonal, column, 0.0), axis=0, keepdims=True)

    def unpack(packed):
        return jnp.sum(jnp.where(diagonal, packed, 0.0), axis=1, keepdims=True)

    loads[0].wait()
    middle = coarse[...]
    edge_out[0] = pack(middle[:, 0:1])
    edge_out[1] = pack(middle[:, depth - 1 : depth])

    sides = [jnp.where(place > 0, 1, 0) + jnp.where(place < size - 1, 1, 0)
             for place, size in ((ang, n_ang), (rad, n_rad))]
    pl.semaphore_wait(barrier, sides[0] * (sides[1] + 1) + n_rad - 1)
    for n, (du, dz) in enumerate(AROUND):
        pl.when(exists(du, dz))(halo_copies[n].start)

    for load in loads[1:]:
        load.wait()

    place = lax.broadcasted_iota(jnp.int32, (slots, depth), 1)
    slot = lax.broadcasted_iota(jnp.int32, (slots, depth), 0)
    group, member = place // cols, place % cols
    order = (group // 2) * (2 * cols) + 2 * member + group % 2

    def wide(ref):
        return jnp.concatenate([ref[0], ref[1]], axis=1)

    def picked(values, index):
        return jnp.take_along_axis(values, index, axis=1, mode="promise_in_bounds")

    counts = jnp.concatenate([count[0:1], count[1:2]], axis=1)
    inverse = picked(jnp.where(slot < counts, wide(isig), 0.0), order)
    live = inverse > 0.0
    observed = picked(wide(obs), order)
    local = picked(wide(bins), order) - rad * (2 * depth)

    evens = (2 * lane) % depth + lane // half
    odds = (2 * lane + 1) % depth - lane // half
    children = [None] * 8
    for i in range(2):
        for j in range(2):
            low = picked(excite[0, i, pl.ds(j, cols, stride=2), :], evens)
            high = picked(excite[1, i, pl.ds(j, cols, stride=2), :], odds)
            q = 4 * i + 2 * j
            children[q] = jnp.where(lane < half, low, high)
            children[q + 1] = pltpu.roll(jnp.where(lane < half, high, low), half, 1)
            blocks[q] = children[q]
            blocks[q + 1] = children[q + 1]
    fine = []
    for q in range(8):
        total = mixing[q, 0:1, :] * children[0]
        for p in range(1, 8):
            total = total + mixing[q, p : p + 1, :] * children[p]
        fine.append(total)

    blank = jnp.zeros((PAD, depth), f32)
    for u in range(3):
        for w in range(3):
            windows[u, w, 0:PAD] = blank
            windows[u, w, PAD + cols : 2 * PAD + cols] = blank
    for q in range(8):
        slopes[q, 0:PAD] = blank
        slopes[q, PAD + cols : 2 * PAD + cols] = blank

    def gather(u, base):
        near, far = unpack(halo_edges[0, u]), unpack(halo_edges[1, u])
        inner = pl.ds(PAD, cols)
        windows[u, 0, inner] = jnp.where(lane == 0, near, pltpu.roll(base, 1, 1))
        windows[u, 1, inner] = base
        windows[u, 2, inner] = jnp.where(lane == depth - 1, far, pltpu.roll(base, depth - 1, 1))

    def spread(u, ws, fine):
        for v in range(3):
            for w in ws:
                window = windows[u, w, PAD - 1 + v : PAD - 1 + v + cols, :]
                t = 9 * u + 3 * v + w
                fine = [
                    fine[q] + weights[t, q : q + 1, :] * window for q in range(8)
                ]
        return fine

    windows[1, 1, PAD : PAD + cols] = middle
    fine = spread(1, (1,), fine)
    for n, (du, dz) in enumerate(AROUND):
        pl.when(exists(-du, -dz))(halo_copies[n].wait_recv)
    gather(1, middle)
    gather(0, halo_rows[0])
    gather(2, halo_rows[1])
    fine = spread(1, (0, 2), fine)
    fine = spread(0, (0, 1, 2), fine)
    fine = spread(2, (0, 1, 2), fine)
    for q in range(8):
        dens[q] = jnp.exp(fine[q])

    pixels = 4 * cols
    ladder = 2 * lax.broadcasted_iota(jnp.int32, (depth, pixels), 0)
    first = jnp.concatenate([dens[q] for q in range(0, 8, 2)], axis=0).T
    second = jnp.concatenate([dens[q] for q in range(1, 8, 2)], axis=0).T
    for m in range(slots):
        limit = local[m : m + 1, :]
        mine[m : m + 1, :] = jnp.sum(
            jnp.where(ladder <= limit, first, 0.0) + jnp.where(ladder < limit, second, 0.0),
            axis=0,
            keepdims=True,
        )
    part_copies = [
        pltpu.make_async_remote_copy(
            src_ref=mine, dst_ref=parts.at[k - 1], send_sem=part_send.at[k - 1],
            recv_sem=part_recv.at[k - 1], device_id=peer(k), device_id_type=MESH,
        )
        for k in range(1, n_rad)
    ]
    for copy in part_copies:
        copy.start()
    for copy in part_copies:
        copy.wait_recv()
    pred = mine[...]
    for k in range(1, n_rad):
        pred = pred + parts[k - 1]
    res = jnp.where(live, (step_len * pred - observed) * inverse, 0.0)
    terms = res * inverse

    first = jnp.zeros((depth, pixels), f32)
    second = jnp.zeros((depth, pixels), f32)
    for m in range(slots):
        limit, term = local[m : m + 1, :], terms[m : m + 1, :]
        first = first + jnp.where(ladder <= limit, term, 0.0)
        second = second + jnp.where(ladder < limit, term, 0.0)
    first, second = first.T, second.T
    for q in range(8):
        suffix = (first, second)[q % 2][(q // 2) * cols : (q // 2 + 1) * cols]
        slopes[q, PAD : PAD + cols] = dens[q] * step_len * suffix

    def collect(u):
        sums = [None] * 3
        for v in range(3):
            for q in range(8):
                window = slopes[q, PAD + 1 - v : PAD + 1 - v + cols, :]
                for w in range(3):
                    term = weights[9 * u + 3 * v + w, q : q + 1, :] * window
                    sums[w] = term if sums[w] is None else sums[w] + term
        back_edges_out[0, u] = pack(sums[0][:, 0:1])
        back_edges_out[1, u] = pack(sums[2][:, depth - 1 : depth])
        low = jnp.where(lane == depth - 1, 0.0, pltpu.roll(sums[0], depth - 1, 1))
        high = jnp.where(lane == 0, 0.0, pltpu.roll(sums[2], 1, 1))
        return sums[1] + low + high

    own = None
    for u in (0, 2, 1):
        result = collect(u)
        if u == 1:
            own = result
        else:
            back_rows_out[u // 2] = result
        for n, (du, dz) in enumerate(AROUND):
            if du == u - 1:
                pl.when(exists(du, dz))(back_copies[n].start)

    grads = []
    for p in range(8):
        total = blocks[p]
        for q in range(8):
            total = total + mixing[q, p : p + 1, :] * slopes[q, PAD : PAD + cols, :]
        grads.append(total)
    even_lane = lane % 2 == 0
    for i in range(2):
        for j in range(2):
            q = 4 * i + 2 * j
            for side in range(2):
                index = side * half + lane // 2
                out_excite[side, i, pl.ds(j, cols, stride=2), :] = jnp.where(
                    even_lane, picked(grads[q], index), picked(grads[q + 1], index)
                )
    stores = [
        pltpu.make_async_copy(
            out_excite.at[side],
            grad_excite_hbm.at[:, :, pl.ds(side * depth, depth)],
            store_sem.at[side],
        )
        for side in range(2)
    ]
    for store in stores:
        store.start()

    for n, (du, dz) in enumerate(AROUND):
        pl.when(exists(-du, -dz))(back_copies[n].wait_recv)
    near = unpack(back_edges[0, 0] + back_edges[0, 1] + back_edges[0, 2])
    far = unpack(back_edges[1, 0] + back_edges[1, 1] + back_edges[1, 2])
    own = own + back_rows[0] + back_rows[1]
    own = own + jnp.where(lane == 0, near, 0.0) + jnp.where(lane == depth - 1, far, 0.0)
    out_coarse[...] = own
    stores.append(pltpu.make_async_copy(out_coarse, grad_coarse_hbm, store_sem.at[2]))
    stores[-1].start()
    for n, (du, dz) in enumerate(AROUND):
        pl.when(exists(du, dz))(halo_copies[n].wait_send)
        pl.when(exists(du, dz))(back_copies[n].wait_send)
    for copy in part_copies:
        copy.wait_send()
    for store in stores:
        store.wait()


def per_device(coarse, excite, kernels, mixing, star_bin, star_count, star_obs, star_isig):
    samples, rows, cols, depth = coarse.shape
    slots = star_bin.shape[2]
    n_ang, n_rad = lax.axis_size("ang"), lax.axis_size("rad")
    assert samples == 1 and rows == 1 and 4 * cols == depth
    f32 = jnp.float32
    vmem, dma = pltpu.VMEM, pltpu.SemaphoreType.DMA
    anywhere = pl.BlockSpec(memory_space=pl.ANY)
    padded = cols + 2 * PAD
    swap = lambda stars: jnp.swapaxes(stars, 1, 2)
    grad_excite, grad_coarse = pl.pallas_call(
        functools.partial(kernel, n_ang, n_rad),
        out_shape=[
            jax.ShapeDtypeStruct(excite.shape[1:], f32),
            jax.ShapeDtypeStruct((cols, depth), f32),
        ],
        in_specs=[anywhere] * 8,
        out_specs=[anywhere] * 2,
        scratch_shapes=[
            vmem((cols, depth), f32),
            vmem((2, 2, 2 * cols, depth), f32),
            vmem((27, 8, depth), f32),
            vmem((8, 8, depth), f32),
            vmem((2, slots, 2 * cols), jnp.int32),
            vmem((2, 2 * cols), jnp.int32),
            vmem((2, slots, 2 * cols), f32),
            vmem((2, slots, 2 * cols), f32),
            vmem((2, 1, depth), f32),
            vmem((2, cols, depth), f32),
            vmem((2, 3, 1, depth), f32),
            vmem((3, 3, padded, depth), f32),
            vmem((8, cols, depth), f32),
            vmem((8, cols, depth), f32),
            vmem((slots, depth), f32),
            vmem((n_rad - 1, slots, depth), f32),
            vmem((8, padded, depth), f32),
            vmem((2, cols, depth), f32),
            vmem((2, 3, 1, depth), f32),
            vmem((2, cols, depth), f32),
            vmem((2, 3, 1, depth), f32),
            vmem((2, 2, 2 * cols, depth), f32),
            vmem((cols, depth), f32),
            dma((9,)),
            dma((8,)),
            dma((8,)),
            dma((n_rad - 1,)),
            dma((n_rad - 1,)),
            dma((8,)),
            dma((8,)),
            dma((3,)),
        ],
        compiler_params=pltpu.CompilerParams(collective_id=0, has_side_effects=True),
    )(
        coarse[0, 0],
        excite[0],
        kernels,
        mixing,
        swap(star_bin),
        star_count,
        swap(star_obs),
        swap(star_isig),
    )
    return grad_excite[None], grad_coarse[None, None]


def solution(mesh):
    in_specs = (
        P(None, "ang", None, "rad"),
        P(None, "ang", None, "rad"),
        P(),
        P(),
        P("ang", None, None),
        P("ang", None),
        P("ang", None, None),
        P("ang", None, None),
    )
    out_specs = (P(None, "ang", None, "rad"), P(None, "ang", None, "rad"))
    return jax.shard_map(
        per_device, mesh=mesh, in_specs=in_specs, out_specs=out_specs, check_vma=False
    )
```

```python
import functools

import jax
import jax.numpy as jnp
from jax import lax
from jax.experimental import pallas as pl
from jax.experimental.pallas import tpu as pltpu
from jax.sharding import PartitionSpec as P

MESH = pl.DeviceIdType.MESH
AROUND = [(du, dz) for du in (-1, 0, 1) for dz in (-1, 0, 1) if (du, dz) != (0, 0)]
PAD = 8


def kernel(
    n_ang,
    n_rad,
    coarse_hbm,
    excite_hbm,
    weights_hbm,
    mixing_hbm,
    bin_hbm,
    count_hbm,
    obs_hbm,
    isig_hbm,
    out_excite,
    out_coarse,
    coarse,
    excite,
    weights,
    mixing,
    bins,
    count,
    obs,
    isig,
    edge_out,
    halo_rows,
    halo_edges,
    windows,
    blocks,
    dens,
    mine,
    parts,
    slopes,
    back_rows_out,
    back_edges_out,
    back_rows,
    back_edges,
    load_sem,
    halo_send,
    halo_recv,
    part_send,
    part_recv,
    back_send,
    back_recv,
):
    ang = lax.axis_index("ang")
    rad = lax.axis_index("rad")
    cols, depth = coarse.shape
    slots = mine.shape[0]
    half = depth // 2
    step_len = 1.0 / (2 * depth * n_rad)
    f32 = jnp.float32

    def exists(du, dz):
        there = None
        for shift, place, size in ((du, ang, n_ang), (dz, rad, n_rad)):
            if shift == 0:
                continue
            ok = place > 0 if shift < 0 else place < size - 1
            there = ok if there is None else jnp.logical_and(there, ok)
        return there

    def at(du, dz):
        return {"ang": ang + du, "rad": rad + dz}

    def peer(k):
        return {"ang": ang, "rad": lax.rem(rad + k, n_rad)}

    here = pl.ds(pl.multiple_of(rad * depth, depth), depth)
    pairs = [
        (coarse_hbm, coarse),
        (excite_hbm.at[:, :, pl.ds(0, depth)], excite.at[0]),
        (excite_hbm.at[:, :, pl.ds(depth, depth)], excite.at[1]),
        (mixing_hbm.at[:, :, here], mixing),
        (weights_hbm.at[:, :, here], weights),
        (bin_hbm, bins),
        (count_hbm, count),
        (obs_hbm, obs),
        (isig_hbm, isig),
    ]
    loads = [
        pltpu.make_async_copy(source, target, load_sem.at[n])
        for n, (source, target) in enumerate(pairs)
    ]
    for load in loads:
        load.start()

    barrier = pltpu.get_barrier_semaphore()
    beside = [(du, dz) for du, dz in AROUND if du != 0]
    for du, dz in beside:

        @pl.when(exists(du, dz))
        def _():
            pl.semaphore_signal(barrier, inc=1, device_id=at(du, dz), device_id_type=MESH)

    for k in range(1, n_rad):
        pl.semaphore_signal(barrier, inc=1, device_id=peer(k), device_id_type=MESH)

    rows_of = lambda du: 0 if du < 0 else 1
    halo_copies, back_copies = [], []
    for n, (du, dz) in enumerate(AROUND):
        if dz == 0:
            source, target = coarse, halo_rows.at[rows_of(-du)]
            back_source, back_target = back_rows_out.at[rows_of(du)], back_rows.at[rows_of(-du)]
        else:
            source, target = edge_out.at[rows_of(dz)], halo_edges.at[rows_of(-dz), 1 - du]
            back_source = back_edges_out.at[rows_of(dz), 1 + du]
            back_target = back_edges.at[rows_of(-dz), 1 - du]
        halo_copies.append(
            pltpu.make_async_remote_copy(
                src_ref=source, dst_ref=target, send_sem=halo_send.at[n],
                recv_sem=halo_recv.at[n], device_id=at(du, dz), device_id_type=MESH,
            )
        )
        back_copies.append(
            pltpu.make_async_remote_copy(
                src_ref=back_source, dst_ref=back_target, send_sem=back_send.at[n],
                recv_sem=back_recv.at[n], device_id=at(du, dz), device_id_type=MESH,
            )
        )

        @pl.when(jnp.logical_not(exists(-du, -dz)))
        def _():
            target[...] = jnp.zeros(target.shape, f32)
            back_target[...] = jnp.zeros(back_target.shape, f32)

    lane = lax.broadcasted_iota(jnp.int32, (cols, depth), 1)
    row = lax.broadcasted_iota(jnp.int32, (cols, depth), 0)
    diagonal = lane == row

    def pack(column):
        return jnp.sum(jnp.where(diagonal, column, 0.0), axis=0, keepdims=True)

    def unpack(packed):
        return jnp.sum(jnp.where(diagonal, packed, 0.0), axis=1, keepdims=True)

    loads[0].wait()
    middle = coarse[...]
    edge_out[0] = pack(middle[:, 0:1])
    edge_out[1] = pack(middle[:, depth - 1 : depth])

    for load in loads[1:]:
        load.wait()

    place = lax.broadcasted_iota(jnp.int32, (slots, depth), 1)
    slot = lax.broadcasted_iota(jnp.int32, (slots, depth), 0)
    group, member = place // cols, place % cols
    order = (group // 2) * (2 * cols) + 2 * member + group % 2

    def wide(ref):
        return jnp.concatenate([ref[0], ref[1]], axis=1)

    def picked(values, index):
        return jnp.take_along_axis(values, index, axis=1, mode="promise_in_bounds")

    counts = jnp.concatenate([count[0:1], count[1:2]], axis=1)
    inverse = picked(jnp.where(slot < counts, wide(isig), 0.0), order)
    live = inverse > 0.0
    observed = picked(wide(obs), order)
    local = picked(wide(bins), order) - rad * (2 * depth)

    evens = (2 * lane) % depth + lane // half
    odds = (2 * lane + 1) % depth - lane // half
    children = [None] * 8
    for i in range(2):
        for j in range(2):
            low = picked(excite[0, i, pl.ds(j, cols, stride=2), :], evens)
            high = picked(excite[1, i, pl.ds(j, cols, stride=2), :], odds)
            q = 4 * i + 2 * j
            children[q] = jnp.where(lane < half, low, high)
            children[q + 1] = pltpu.roll(jnp.where(lane < half, high, low), half, 1)
            blocks[q] = children[q]
            blocks[q + 1] = children[q + 1]
    fine = []
    for q in range(8):
        total = mixing[q, 0:1, :] * children[0]
        for p in range(1, 8):
            total = total + mixing[q, p : p + 1, :] * children[p]
        fine.append(total)

    sides = [jnp.where(place > 0, 1, 0) + jnp.where(place < size - 1, 1, 0)
             for place, size in ((ang, n_ang), (rad, n_rad))]
    pl.semaphore_wait(barrier, sides[0] * (sides[1] + 1) + n_rad - 1)
    for n, (du, dz) in enumerate(AROUND):
        pl.when(exists(du, dz))(halo_copies[n].start)

    blank = jnp.zeros((PAD, depth), f32)
    for u in range(3):
        for w in range(3):
            windows[u, w, 0:PAD] = blank
            windows[u, w, PAD + cols : 2 * PAD + cols] = blank
    for q in range(8):
        slopes[q, 0:PAD] = blank
        slopes[q, PAD + cols : 2 * PAD + cols] = blank

    def gather(u, base):
        near, far = unpack(halo_edges[0, u]), unpack(halo_edges[1, u])
        inner = pl.ds(PAD, cols)
        windows[u, 0, inner] = jnp.where(lane == 0, near, pltpu.roll(base, 1, 1))
        windows[u, 1, inner] = base
        windows[u, 2, inner] = jnp.where(lane == depth - 1, far, pltpu.roll(base, depth - 1, 1))

    def spread(u, ws, fine):
        for v in range(3):
            for w in ws:
                window = windows[u, w, PAD - 1 + v : PAD - 1 + v + cols, :]
                t = 9 * u + 3 * v + w
                fine = [
                    fine[q] + weights[t, q : q + 1, :] * window for q in range(8)
                ]
        return fine

    windows[1, 1, PAD : PAD + cols] = middle
    fine = spread(1, (1,), fine)
    for n, (du, dz) in enumerate(AROUND):
        pl.when(exists(-du, -dz))(halo_copies[n].wait_recv)
    gather(1, middle)
    gather(0, halo_rows[0])
    gather(2, halo_rows[1])
    fine = spread(1, (0, 2), fine)
    fine = spread(0, (0, 1, 2), fine)
    fine = spread(2, (0, 1, 2), fine)
    for q in range(8):
        dens[q] = jnp.exp(fine[q])

    pixels = 4 * cols
    ladder = 2 * lax.broadcasted_iota(jnp.int32, (depth, pixels), 0)
    first = jnp.concatenate([dens[q] for q in range(0, 8, 2)], axis=0).T
    second = jnp.concatenate([dens[q] for q in range(1, 8, 2)], axis=0).T
    for m in range(slots):
        limit = local[m : m + 1, :]
        mine[m : m + 1, :] = jnp.sum(
            jnp.where(ladder <= limit, first, 0.0) + jnp.where(ladder < limit, second, 0.0),
            axis=0,
            keepdims=True,
        )
    part_copies = [
        pltpu.make_async_remote_copy(
            src_ref=mine, dst_ref=parts.at[k - 1], send_sem=part_send.at[k - 1],
            recv_sem=part_recv.at[k - 1], device_id=peer(k), device_id_type=MESH,
        )
        for k in range(1, n_rad)
    ]
    for copy in part_copies:
        copy.start()
    for copy in part_copies:
        copy.wait_recv()
    pred = mine[...]
    for k in range(1, n_rad):
        pred = pred + parts[k - 1]
    res = jnp.where(live, (step_len * pred - observed) * inverse, 0.0)
    terms = res * inverse

    first = jnp.zeros((depth, pixels), f32)
    second = jnp.zeros((depth, pixels), f32)
    for m in range(slots):
        limit, term = local[m : m + 1, :], terms[m : m + 1, :]
        first = first + jnp.where(ladder <= limit, term, 0.0)
        second = second + jnp.where(ladder < limit, term, 0.0)
    first, second = first.T, second.T
    for q in range(8):
        suffix = (first, second)[q % 2][(q // 2) * cols : (q // 2 + 1) * cols]
        slopes[q, PAD : PAD + cols] = dens[q] * step_len * suffix

    def collect(u):
        sums = [None] * 3
        for v in range(3):
            for q in range(8):
                window = slopes[q, PAD + 1 - v : PAD + 1 - v + cols, :]
                for w in range(3):
                    term = weights[9 * u + 3 * v + w, q : q + 1, :] * window
                    sums[w] = term if sums[w] is None else sums[w] + term
        back_edges_out[0, u] = pack(sums[0][:, 0:1])
        back_edges_out[1, u] = pack(sums[2][:, depth - 1 : depth])
        low = jnp.where(lane == depth - 1, 0.0, pltpu.roll(sums[0], depth - 1, 1))
        high = jnp.where(lane == 0, 0.0, pltpu.roll(sums[2], 1, 1))
        return sums[1] + low + high

    own = None
    for u in (0, 2, 1):
        result = collect(u)
        if u == 1:
            own = result
        else:
            back_rows_out[u // 2] = result
        for n, (du, dz) in enumerate(AROUND):
            if du == u - 1:
                pl.when(exists(du, dz))(back_copies[n].start)

    grads = []
    for p in range(8):
        total = blocks[p]
        for q in range(8):
            total = total + mixing[q, p : p + 1, :] * slopes[q, PAD : PAD + cols, :]
        grads.append(total)
    even_lane = lane % 2 == 0
    for i in range(2):
        for j in range(2):
            q = 4 * i + 2 * j
            for side in range(2):
                index = side * half + lane // 2
                out_excite[side, i, pl.ds(j, cols, stride=2), :] = jnp.where(
                    even_lane, picked(grads[q], index), picked(grads[q + 1], index)
                )
    for n, (du, dz) in enumerate(AROUND):
        pl.when(exists(-du, -dz))(back_copies[n].wait_recv)
    near = unpack(back_edges[0, 0] + back_edges[0, 1] + back_edges[0, 2])
    far = unpack(back_edges[1, 0] + back_edges[1, 1] + back_edges[1, 2])
    own = own + back_rows[0] + back_rows[1]
    own = own + jnp.where(lane == 0, near, 0.0) + jnp.where(lane == depth - 1, far, 0.0)
    out_coarse[...] = own
    for n, (du, dz) in enumerate(AROUND):
        pl.when(exists(du, dz))(halo_copies[n].wait_send)
        pl.when(exists(du, dz))(back_copies[n].wait_send)
    for copy in part_copies:
        copy.wait_send()


def write(halves, block, grad_excite, grad_coarse, sem):
    depth = block.shape[1]
    pairs = [(halves.at[side], grad_excite.at[:, :, pl.ds(side * depth, depth)]) for side in range(2)]
    pairs.append((block, grad_coarse))
    copies = [
        pltpu.make_async_copy(source, target, sem.at[n])
        for n, (source, target) in enumerate(pairs)
    ]
    for copy in copies:
        copy.start()
    for copy in copies:
        copy.wait()


def per_device(coarse, excite, kernels, mixing, star_bin, star_count, star_obs, star_isig):
    samples, rows, cols, depth = coarse.shape
    slots = star_bin.shape[2]
    n_ang, n_rad = lax.axis_size("ang"), lax.axis_size("rad")
    assert samples == 1 and rows == 1 and 4 * cols == depth
    f32 = jnp.float32
    vmem, dma = pltpu.VMEM, pltpu.SemaphoreType.DMA
    anywhere = pl.BlockSpec(memory_space=pl.ANY)
    padded = cols + 2 * PAD
    swap = lambda stars: jnp.swapaxes(stars, 1, 2)
    results = pl.pallas_call(
        functools.partial(kernel, n_ang, n_rad),
        out_shape=[vmem((2, 2, 2 * cols, depth), f32), vmem((cols, depth), f32)],
        in_specs=[pl.BlockSpec(memory_space=pltpu.HBM)] * 8,
        out_specs=[pl.BlockSpec(memory_space=vmem)] * 2,
        scratch_shapes=[
            vmem((cols, depth), f32),
            vmem((2, 2, 2 * cols, depth), f32),
            vmem((27, 8, depth), f32),
            vmem((8, 8, depth), f32),
            vmem((2, slots, 2 * cols), jnp.int32),
            vmem((2, 2 * cols), jnp.int32),
            vmem((2, slots, 2 * cols), f32),
            vmem((2, slots, 2 * cols), f32),
            vmem((2, 1, depth), f32),
            vmem((2, cols, depth), f32),
            vmem((2, 3, 1, depth), f32),
            vmem((3, 3, padded, depth), f32),
            vmem((8, cols, depth), f32),
            vmem((8, cols, depth), f32),
            vmem((slots, depth), f32),
            vmem((n_rad - 1, slots, depth), f32),
            vmem((8, padded, depth), f32),
            vmem((2, cols, depth), f32),
            vmem((2, 3, 1, depth), f32),
            vmem((2, cols, depth), f32),
            vmem((2, 3, 1, depth), f32),
            dma((9,)),
            dma((8,)),
            dma((8,)),
            dma((n_rad - 1,)),
            dma((n_rad - 1,)),
            dma((8,)),
            dma((8,)),
        ],
        compiler_params=pltpu.CompilerParams(
            collective_id=0, has_side_effects=True, vmem_limit_bytes=8 << 20
        ),
    )(
        *(
            pltpu.with_memory_space_constraint(argument, pltpu.HBM)
            for argument in (
                coarse[0, 0],
                excite[0],
                kernels,
                mixing,
                swap(star_bin),
                star_count,
                swap(star_obs),
                swap(star_isig),
            )
        )
    )
    grad_excite, grad_coarse = pl.pallas_call(
        write,
        out_shape=[
            jax.ShapeDtypeStruct(excite.shape[1:], f32),
            jax.ShapeDtypeStruct((cols, depth), f32),
        ],
        in_specs=[anywhere] * 2,
        out_specs=[pl.BlockSpec(memory_space=pltpu.HBM)] * 2,
        scratch_shapes=[dma((3,))],
        compiler_params=pltpu.CompilerParams(vmem_limit_bytes=1 << 20),
    )(*results)
    return grad_excite[None], grad_coarse[None, None]


def solution(mesh):
    in_specs = (
        P(None, "ang", None, "rad"),
        P(None, "ang", None, "rad"),
        P(),
        P(),
        P("ang", None, None),
        P("ang", None),
        P("ang", None, None),
        P("ang", None, None),
    )
    out_specs = (P(None, "ang", None, "rad"), P(None, "ang", None, "rad"))
    return jax.shard_map(
        per_device, mesh=mesh, in_specs=in_specs, out_specs=out_specs, check_vma=False
    )
```

```python
import functools

import jax
import jax.numpy as jnp
from jax import lax
from jax.experimental import pallas as pl
from jax.experimental.pallas import tpu as pltpu
from jax.sharding import PartitionSpec as P

MESH = pl.DeviceIdType.MESH
AROUND = [(du, dz) for du in (-1, 0, 1) for dz in (-1, 0, 1) if (du, dz) != (0, 0)]
AROUND.sort(key=lambda step: -abs(step[0]) - abs(step[1]))
PAD = 8


def kernel(
    n_ang,
    n_rad,
    coarse_hbm,
    excite_hbm,
    weights_hbm,
    mixing_hbm,
    bin_hbm,
    count_hbm,
    obs_hbm,
    isig_hbm,
    out_excite,
    out_coarse,
    coarse,
    excite,
    weights,
    mixing,
    bins,
    count,
    obs,
    isig,
    edge_out,
    halo_rows,
    halo_edges,
    windows,
    blocks,
    dens,
    mine,
    parts,
    slopes,
    back_rows_out,
    back_edges_out,
    back_rows,
    back_edges,
    load_sem,
    halo_send,
    halo_recv,
    part_send,
    part_recv,
    back_send,
    back_recv,
):
    ang = lax.axis_index("ang")
    rad = lax.axis_index("rad")
    cols, depth = coarse.shape
    slots = mine.shape[0]
    half = depth // 2
    step_len = 1.0 / (2 * depth * n_rad)
    f32 = jnp.float32

    def exists(du, dz):
        there = None
        for shift, place, size in ((du, ang, n_ang), (dz, rad, n_rad)):
            if shift == 0:
                continue
            ok = place > 0 if shift < 0 else place < size - 1
            there = ok if there is None else jnp.logical_and(there, ok)
        return there

    def at(du, dz):
        return {"ang": ang + du, "rad": rad + dz}

    def peer(k):
        return {"ang": ang, "rad": lax.rem(rad + k, n_rad)}

    here = pl.ds(pl.multiple_of(rad * depth, depth), depth)
    pairs = [
        (coarse_hbm, coarse),
        (excite_hbm.at[:, :, pl.ds(0, depth)], excite.at[0]),
        (excite_hbm.at[:, :, pl.ds(depth, depth)], excite.at[1]),
        (mixing_hbm.at[:, :, here], mixing),
        (weights_hbm.at[:, :, here], weights),
        (bin_hbm, bins),
        (count_hbm, count),
        (obs_hbm, obs),
        (isig_hbm, isig),
    ]
    loads = [
        pltpu.make_async_copy(source, target, load_sem.at[n])
        for n, (source, target) in enumerate(pairs)
    ]
    loads[0].start()

    barrier = pltpu.get_barrier_semaphore()
    beside = [(du, dz) for du, dz in AROUND if du != 0]
    for du, dz in beside:

        @pl.when(exists(du, dz))
        def _():
            pl.semaphore_signal(barrier, inc=1, device_id=at(du, dz), device_id_type=MESH)

    for k in range(1, n_rad):
        pl.semaphore_signal(barrier, inc=1, device_id=peer(k), device_id_type=MESH)
    for load in loads[1:]:
        load.start()

    rows_of = lambda du: 0 if du < 0 else 1
    halo_copies, back_copies, targets = [], [], []
    for n, (du, dz) in enumerate(AROUND):
        if dz == 0:
            source, target = coarse, halo_rows.at[rows_of(-du)]
            back_source, back_target = back_rows_out.at[rows_of(du)], back_rows.at[rows_of(-du)]
        else:
            source, target = edge_out.at[rows_of(dz)], halo_edges.at[rows_of(-dz), 1 - du]
            back_source = back_edges_out.at[rows_of(dz), 1 + du]
            back_target = back_edges.at[rows_of(-dz), 1 - du]
        halo_copies.append(
            pltpu.make_async_remote_copy(
                src_ref=source, dst_ref=target, send_sem=halo_send.at[n],
                recv_sem=halo_recv.at[n], device_id=at(du, dz), device_id_type=MESH,
            )
        )
        back_copies.append(
            pltpu.make_async_remote_copy(
                src_ref=back_source, dst_ref=back_target, send_sem=back_send.at[n],
                recv_sem=back_recv.at[n], device_id=at(du, dz), device_id_type=MESH,
            )
        )
        targets.append((target, back_target))

    lane = lax.broadcasted_iota(jnp.int32, (cols, depth), 1)
    row = lax.broadcasted_iota(jnp.int32, (cols, depth), 0)
    diagonal = lane == row

    def pack(column):
        return jnp.sum(jnp.where(diagonal, column, 0.0), axis=0, keepdims=True)

    def unpack(packed):
        return jnp.sum(jnp.where(diagonal, packed, 0.0), axis=1, keepdims=True)

    loads[0].wait()
    middle = coarse[...]
    edge_out[0] = pack(middle[:, 0:1])
    edge_out[1] = pack(middle[:, depth - 1 : depth])

    sides = [jnp.where(place > 0, 1, 0) + jnp.where(place < size - 1, 1, 0)
             for place, size in ((ang, n_ang), (rad, n_rad))]
    pl.semaphore_wait(barrier, sides[0] * (sides[1] + 1) + n_rad - 1)
    for n, (du, dz) in enumerate(AROUND):
        pl.when(exists(du, dz))(halo_copies[n].start)

    for (du, dz), (target, back_target) in zip(AROUND, targets):

        @pl.when(jnp.logical_not(exists(-du, -dz)))
        def _():
            target[...] = jnp.zeros(target.shape, f32)
            back_target[...] = jnp.zeros(back_target.shape, f32)

    for load in loads[1:]:
        load.wait()

    place = lax.broadcasted_iota(jnp.int32, (slots, depth), 1)
    slot = lax.broadcasted_iota(jnp.int32, (slots, depth), 0)
    group, member = place // cols, place % cols
    order = (group // 2) * (2 * cols) + 2 * member + group % 2

    def wide(ref):
        return jnp.concatenate([ref[0], ref[1]], axis=1)

    def picked(values, index):
        return jnp.take_along_axis(values, index, axis=1, mode="promise_in_bounds")

    counts = jnp.concatenate([count[0:1], count[1:2]], axis=1)
    inverse = picked(jnp.where(slot < counts, wide(isig), 0.0), order)
    live = inverse > 0.0
    observed = picked(wide(obs), order)
    local = picked(wide(bins), order) - rad * (2 * depth)

    evens = (2 * lane) % depth + lane // half
    odds = (2 * lane + 1) % depth - lane // half
    children = [None] * 8
    for i in range(2):
        for j in range(2):
            low = picked(excite[0, i, pl.ds(j, cols, stride=2), :], evens)
            high = picked(excite[1, i, pl.ds(j, cols, stride=2), :], odds)
            q = 4 * i + 2 * j
            children[q] = jnp.where(lane < half, low, high)
            children[q + 1] = pltpu.roll(jnp.where(lane < half, high, low), half, 1)
            blocks[q] = children[q]
            blocks[q + 1] = children[q + 1]
    fine = []
    for q in range(8):
        total = mixing[q, 0:1, :] * children[0]
        for p in range(1, 8):
            total = total + mixing[q, p : p + 1, :] * children[p]
        fine.append(total)

    blank = jnp.zeros((PAD, depth), f32)
    for u in range(3):
        for w in range(3):
            windows[u, w, 0:PAD] = blank
            windows[u, w, PAD + cols : 2 * PAD + cols] = blank
    for q in range(8):
        slopes[q, 0:PAD] = blank
        slopes[q, PAD + cols : 2 * PAD + cols] = blank

    def gather(u, base):
        near, far = unpack(halo_edges[0, u]), unpack(halo_edges[1, u])
        inner = pl.ds(PAD, cols)
        windows[u, 0, inner] = jnp.where(lane == 0, near, pltpu.roll(base, 1, 1))
        windows[u, 2, inner] = jnp.where(lane == depth - 1, far, pltpu.roll(base, depth - 1, 1))

    def spread(u, ws, fine):
        for v in range(3):
            for w in ws:
                window = windows[u, w, PAD - 1 + v : PAD - 1 + v + cols, :]
                t = 9 * u + 3 * v + w
                fine = [
                    fine[q] + weights[t, q : q + 1, :] * window for q in range(8)
                ]
        return fine

    windows[1, 1, PAD : PAD + cols] = middle
    fine = spread(1, (1,), fine)
    def arrived(choose):
        for n, (du, dz) in enumerate(AROUND):
            if choose(du, dz):
                pl.when(exists(-du, -dz))(halo_copies[n].wait_recv)

    arrived(lambda du, dz: du == 0)
    gather(1, middle)
    fine = spread(1, (0, 2), fine)
    arrived(lambda du, dz: dz == 0)
    for u in (0, 2):
        windows[u, 1, PAD : PAD + cols] = halo_rows[u // 2]
        fine = spread(u, (1,), fine)
    arrived(lambda du, dz: du != 0 and dz != 0)
    for u in (0, 2):
        gather(u, halo_rows[u // 2])
        fine = spread(u, (0, 2), fine)
    for q in range(8):
        dens[q] = jnp.exp(fine[q])

    pixels = 4 * cols
    ladder = 2 * lax.broadcasted_iota(jnp.int32, (depth, pixels), 0)
    first = jnp.concatenate([dens[q] for q in range(0, 8, 2)], axis=0).T
    second = jnp.concatenate([dens[q] for q in range(1, 8, 2)], axis=0).T
    for m in range(slots):
        limit = local[m : m + 1, :]
        mine[m : m + 1, :] = jnp.sum(
            jnp.where(ladder <= limit, first, 0.0) + jnp.where(ladder < limit, second, 0.0),
            axis=0,
            keepdims=True,
        )
    part_copies = [
        pltpu.make_async_remote_copy(
            src_ref=mine, dst_ref=parts.at[k - 1], send_sem=part_send.at[k - 1],
            recv_sem=part_recv.at[k - 1], device_id=peer(k), device_id_type=MESH,
        )
        for k in range(1, n_rad)
    ]
    for copy in part_copies:
        copy.start()
    for copy in part_copies:
        copy.wait_recv()
    pred = mine[...]
    for k in range(1, n_rad):
        pred = pred + parts[k - 1]
    res = jnp.where(live, (step_len * pred - observed) * inverse, 0.0)
    terms = res * inverse

    first = jnp.zeros((depth, pixels), f32)
    second = jnp.zeros((depth, pixels), f32)
    for m in range(slots):
        limit, term = local[m : m + 1, :], terms[m : m + 1, :]
        first = first + jnp.where(ladder <= limit, term, 0.0)
        second = second + jnp.where(ladder < limit, term, 0.0)
    first, second = first.T, second.T
    for q in range(8):
        suffix = (first, second)[q % 2][(q // 2) * cols : (q // 2 + 1) * cols]
        slopes[q, PAD : PAD + cols] = dens[q] * step_len * suffix

    def collect(u):
        sums = [None] * 3
        for v in range(3):
            for q in range(8):
                window = slopes[q, PAD + 1 - v : PAD + 1 - v + cols, :]
                for w in range(3):
                    term = weights[9 * u + 3 * v + w, q : q + 1, :] * window
                    sums[w] = term if sums[w] is None else sums[w] + term
        back_edges_out[0, u] = pack(sums[0][:, 0:1])
        back_edges_out[1, u] = pack(sums[2][:, depth - 1 : depth])
        low = jnp.where(lane == depth - 1, 0.0, pltpu.roll(sums[0], depth - 1, 1))
        high = jnp.where(lane == 0, 0.0, pltpu.roll(sums[2], 1, 1))
        return sums[1] + low + high

    own = None
    for u in (0, 2, 1):
        result = collect(u)
        if u == 1:
            own = result
        else:
            back_rows_out[u // 2] = result
        for n, (du, dz) in enumerate(AROUND):
            if du == u - 1:
                pl.when(exists(du, dz))(back_copies[n].start)

    grads = []
    for p in range(8):
        total = blocks[p]
        for q in range(8):
            total = total + mixing[q, p : p + 1, :] * slopes[q, PAD : PAD + cols, :]
        grads.append(total)
    even_lane = lane % 2 == 0
    for i in range(2):
        for j in range(2):
            q = 4 * i + 2 * j
            for side in range(2):
                index = side * half + lane // 2
                out_excite[side, i, pl.ds(j, cols, stride=2), :] = jnp.where(
                    even_lane, picked(grads[q], index), picked(grads[q + 1], index)
                )
    for n, (du, dz) in enumerate(AROUND):
        pl.when(exists(-du, -dz))(back_copies[n].wait_recv)
    near = unpack(back_edges[0, 0] + back_edges[0, 1] + back_edges[0, 2])
    far = unpack(back_edges[1, 0] + back_edges[1, 1] + back_edges[1, 2])
    own = own + back_rows[0] + back_rows[1]
    own = own + jnp.where(lane == 0, near, 0.0) + jnp.where(lane == depth - 1, far, 0.0)
    out_coarse[...] = own
    for n, (du, dz) in enumerate(AROUND):
        pl.when(exists(du, dz))(halo_copies[n].wait_send)
        pl.when(exists(du, dz))(back_copies[n].wait_send)
    for copy in part_copies:
        copy.wait_send()


def write(halves, block, grad_excite, grad_coarse, sem):
    depth = block.shape[1]
    pairs = [(halves.at[side], grad_excite.at[:, :, pl.ds(side * depth, depth)]) for side in range(2)]
    pairs.append((block, grad_coarse))
    copies = [
        pltpu.make_async_copy(source, target, sem.at[n])
        for n, (source, target) in enumerate(pairs)
    ]
    for copy in copies:
        copy.start()
    for copy in copies:
        copy.wait()


def per_device(coarse, excite, kernels, mixing, star_bin, star_count, star_obs, star_isig):
    samples, rows, cols, depth = coarse.shape
    slots = star_bin.shape[2]
    n_ang, n_rad = lax.axis_size("ang"), lax.axis_size("rad")
    assert samples == 1 and rows == 1 and 4 * cols == depth
    f32 = jnp.float32
    vmem, dma = pltpu.VMEM, pltpu.SemaphoreType.DMA
    anywhere = pl.BlockSpec(memory_space=pl.ANY)
    padded = cols + 2 * PAD
    swap = lambda stars: jnp.swapaxes(stars, 1, 2)
    results = pl.pallas_call(
        functools.partial(kernel, n_ang, n_rad),
        out_shape=[vmem((2, 2, 2 * cols, depth), f32), vmem((cols, depth), f32)],
        in_specs=[pl.BlockSpec(memory_space=pltpu.HBM)] * 8,
        out_specs=[pl.BlockSpec(memory_space=vmem)] * 2,
        scratch_shapes=[
            vmem((cols, depth), f32),
            vmem((2, 2, 2 * cols, depth), f32),
            vmem((27, 8, depth), f32),
            vmem((8, 8, depth), f32),
            vmem((2, slots, 2 * cols), jnp.int32),
            vmem((2, 2 * cols), jnp.int32),
            vmem((2, slots, 2 * cols), f32),
            vmem((2, slots, 2 * cols), f32),
            vmem((2, 1, depth), f32),
            vmem((2, cols, depth), f32),
            vmem((2, 3, 1, depth), f32),
            vmem((3, 3, padded, depth), f32),
            vmem((8, cols, depth), f32),
            vmem((8, cols, depth), f32),
            vmem((slots, depth), f32),
            vmem((n_rad - 1, slots, depth), f32),
            vmem((8, padded, depth), f32),
            vmem((2, cols, depth), f32),
            vmem((2, 3, 1, depth), f32),
            vmem((2, cols, depth), f32),
            vmem((2, 3, 1, depth), f32),
            dma((9,)),
            dma((8,)),
            dma((8,)),
            dma((n_rad - 1,)),
            dma((n_rad - 1,)),
            dma((8,)),
            dma((8,)),
        ],
        compiler_params=pltpu.CompilerParams(
            collective_id=0, has_side_effects=True, vmem_limit_bytes=8 << 20
        ),
    )(
        *(
            pltpu.with_memory_space_constraint(argument, pltpu.HBM)
            for argument in (
                coarse[0, 0],
                excite[0],
                kernels,
                mixing,
                swap(star_bin),
                star_count,
                swap(star_obs),
                swap(star_isig),
            )
        )
    )
    grad_excite, grad_coarse = pl.pallas_call(
        write,
        out_shape=[
            jax.ShapeDtypeStruct(excite.shape[1:], f32),
            jax.ShapeDtypeStruct((cols, depth), f32),
        ],
        in_specs=[anywhere] * 2,
        out_specs=[pl.BlockSpec(memory_space=pltpu.HBM)] * 2,
        scratch_shapes=[dma((3,))],
        compiler_params=pltpu.CompilerParams(vmem_limit_bytes=1 << 20),
    )(*results)
    return grad_excite[None], grad_coarse[None, None]


def solution(mesh):
    in_specs = (
        P(None, "ang", None, "rad"),
        P(None, "ang", None, "rad"),
        P(),
        P(),
        P("ang", None, None),
        P("ang", None),
        P("ang", None, None),
        P("ang", None, None),
    )
    out_specs = (P(None, "ang", None, "rad"), P(None, "ang", None, "rad"))
    return jax.shard_map(
        per_device, mesh=mesh, in_specs=in_specs, out_specs=out_specs, check_vma=False
    )
```

```python
import functools

import jax
import jax.numpy as jnp
from jax import lax
from jax.experimental import pallas as pl
from jax.experimental.pallas import tpu as pltpu
from jax.sharding import PartitionSpec as P

MESH = pl.DeviceIdType.MESH
AROUND = [(du, dz) for du in (-1, 0, 1) for dz in (-1, 0, 1) if (du, dz) != (0, 0)]
AROUND.sort(key=lambda step: -abs(step[0]) - abs(step[1]))
PAD = 8
UNROLL = 4


def kernel(
    n_ang,
    n_rad,
    coarse_hbm,
    excite_hbm,
    weights_hbm,
    mixing_hbm,
    bin_hbm,
    count_hbm,
    obs_hbm,
    isig_hbm,
    out_excite,
    out_coarse,
    coarse,
    excite,
    weights,
    mixing,
    bins,
    count,
    obs,
    isig,
    edge_out,
    halo_rows,
    halo_edges,
    windows,
    blocks,
    dens,
    mine,
    parts,
    local,
    terms,
    slopes,
    back_rows_out,
    back_edges_out,
    back_rows,
    back_edges,
    load_sem,
    halo_send,
    halo_recv,
    part_send,
    part_recv,
    back_send,
    back_recv,
):
    ang = lax.axis_index("ang")
    rad = lax.axis_index("rad")
    cols, depth = coarse.shape
    slots = mine.shape[0]
    half = depth // 2
    step_len = 1.0 / (2 * depth * n_rad)
    f32 = jnp.float32

    def exists(du, dz):
        there = None
        for shift, place, size in ((du, ang, n_ang), (dz, rad, n_rad)):
            if shift == 0:
                continue
            ok = place > 0 if shift < 0 else place < size - 1
            there = ok if there is None else jnp.logical_and(there, ok)
        return there

    def at(du, dz):
        return {"ang": ang + du, "rad": rad + dz}

    def peer(k):
        return {"ang": ang, "rad": lax.rem(rad + k, n_rad)}

    here = pl.ds(pl.multiple_of(rad * depth, depth), depth)
    pairs = [
        (coarse_hbm, coarse),
        (excite_hbm.at[:, :, pl.ds(0, depth)], excite.at[0]),
        (excite_hbm.at[:, :, pl.ds(depth, depth)], excite.at[1]),
        (mixing_hbm.at[:, :, here], mixing),
        (weights_hbm.at[:, :, here], weights),
        (bin_hbm, bins),
        (count_hbm, count),
        (obs_hbm, obs),
        (isig_hbm, isig),
    ]
    loads = [
        pltpu.make_async_copy(source, target, load_sem.at[n])
        for n, (source, target) in enumerate(pairs)
    ]
    loads[0].start()

    barrier = pltpu.get_barrier_semaphore()
    beside = [(du, dz) for du, dz in AROUND if du != 0]
    for du, dz in beside:

        @pl.when(exists(du, dz))
        def _():
            pl.semaphore_signal(barrier, inc=1, device_id=at(du, dz), device_id_type=MESH)

    for k in range(1, n_rad):
        pl.semaphore_signal(barrier, inc=1, device_id=peer(k), device_id_type=MESH)
    for load in loads[1:]:
        load.start()

    rows_of = lambda du: 0 if du < 0 else 1
    halo_copies, back_copies, targets = [], [], []
    for n, (du, dz) in enumerate(AROUND):
        if dz == 0:
            source, target = coarse, halo_rows.at[rows_of(-du)]
            back_source, back_target = back_rows_out.at[rows_of(du)], back_rows.at[rows_of(-du)]
        else:
            source, target = edge_out.at[rows_of(dz)], halo_edges.at[rows_of(-dz), 1 - du]
            back_source = back_edges_out.at[rows_of(dz), 1 + du]
            back_target = back_edges.at[rows_of(-dz), 1 - du]
        halo_copies.append(
            pltpu.make_async_remote_copy(
                src_ref=source, dst_ref=target, send_sem=halo_send.at[n],
                recv_sem=halo_recv.at[n], device_id=at(du, dz), device_id_type=MESH,
            )
        )
        back_copies.append(
            pltpu.make_async_remote_copy(
                src_ref=back_source, dst_ref=back_target, send_sem=back_send.at[n],
                recv_sem=back_recv.at[n], device_id=at(du, dz), device_id_type=MESH,
            )
        )
        targets.append((target, back_target))

    lane = lax.broadcasted_iota(jnp.int32, (cols, depth), 1)
    row = lax.broadcasted_iota(jnp.int32, (cols, depth), 0)
    diagonal = lane == row

    def pack(column):
        return jnp.sum(jnp.where(diagonal, column, 0.0), axis=0, keepdims=True)

    def unpack(packed):
        return jnp.sum(jnp.where(diagonal, packed, 0.0), axis=1, keepdims=True)

    loads[0].wait()
    middle = coarse[...]
    edge_out[0] = pack(middle[:, 0:1])
    edge_out[1] = pack(middle[:, depth - 1 : depth])

    sides = [jnp.where(place > 0, 1, 0) + jnp.where(place < size - 1, 1, 0)
             for place, size in ((ang, n_ang), (rad, n_rad))]
    pl.semaphore_wait(barrier, sides[0] * (sides[1] + 1) + n_rad - 1)
    for n, (du, dz) in enumerate(AROUND):
        pl.when(exists(du, dz))(halo_copies[n].start)

    for (du, dz), (target, back_target) in zip(AROUND, targets):

        @pl.when(jnp.logical_not(exists(-du, -dz)))
        def _():
            target[...] = jnp.zeros(target.shape, f32)
            back_target[...] = jnp.zeros(back_target.shape, f32)

    for load in loads[1:]:
        load.wait()

    place = lax.broadcasted_iota(jnp.int32, (slots, depth), 1)
    slot = lax.broadcasted_iota(jnp.int32, (slots, depth), 0)
    group, member = place // cols, place % cols
    order = (group // 2) * (2 * cols) + 2 * member + group % 2

    def wide(ref):
        return jnp.concatenate([ref[0], ref[1]], axis=1)

    def picked(values, index):
        return jnp.take_along_axis(values, index, axis=1, mode="promise_in_bounds")

    counts = jnp.concatenate([count[0:1], count[1:2]], axis=1)
    inverse = picked(jnp.where(slot < counts, wide(isig), 0.0), order)
    live = inverse > 0.0
    observed = picked(wide(obs), order)
    local[...] = picked(wide(bins), order) - rad * (2 * depth)

    evens = (2 * lane) % depth + lane // half
    odds = (2 * lane + 1) % depth - lane // half

    def split(i, carry):
        for j in range(2):
            low = picked(excite[0, i, pl.ds(j, cols, stride=2), :], evens)
            high = picked(excite[1, i, pl.ds(j, cols, stride=2), :], odds)
            blocks[4 * i + 2 * j] = jnp.where(lane < half, low, high)
            blocks[4 * i + 2 * j + 1] = pltpu.roll(jnp.where(lane < half, high, low), half, 1)
        return carry

    lax.fori_loop(0, 2, split, 0)

    def mix(p, fine):
        child = blocks[p]
        return tuple(fine[q] + mixing[q, pl.ds(p, 1), :] * child for q in range(8))

    fine = lax.fori_loop(0, 8, mix, tuple(jnp.zeros((cols, depth), f32) for _ in range(8)))

    blank = jnp.zeros((PAD, depth), f32)
    for u in range(3):
        for w in range(3):
            windows[u, w, 0:PAD] = blank
            windows[u, w, PAD + cols : 2 * PAD + cols] = blank
    for q in range(8):
        slopes[q, 0:PAD] = blank
        slopes[q, PAD + cols : 2 * PAD + cols] = blank

    def gather(u, base):
        near, far = unpack(halo_edges[0, u]), unpack(halo_edges[1, u])
        inner = pl.ds(PAD, cols)
        windows[u, 0, inner] = jnp.where(lane == 0, near, pltpu.roll(base, 1, 1))
        windows[u, 1, inner] = base
        windows[u, 2, inner] = jnp.where(lane == depth - 1, far, pltpu.roll(base, depth - 1, 1))

    def spread(u, fine):
        for v in range(3):
            for w in range(3):
                window = windows[u, w, PAD - 1 + v : PAD - 1 + v + cols, :]
                t = 9 * u + 3 * v + w
                fine = tuple(fine[q] + weights[t, q : q + 1, :] * window for q in range(8))
        return fine

    for n, (du, dz) in enumerate(AROUND):
        pl.when(exists(-du, -dz))(halo_copies[n].wait_recv)
    gather(0, halo_rows[0])
    gather(1, middle)
    gather(2, halo_rows[1])
    fine = lax.fori_loop(0, 3, spread, fine)
    for q in range(8):
        dens[q] = jnp.exp(fine[q])

    pixels = 4 * cols
    ladder = 2 * lax.broadcasted_iota(jnp.int32, (depth, pixels), 0)
    first = jnp.concatenate([dens[q] for q in range(0, 8, 2)], axis=0).T
    second = jnp.concatenate([dens[q] for q in range(1, 8, 2)], axis=0).T

    def reach(step, carry):
        for n in range(UNROLL):
            m = pl.ds(step * UNROLL + n, 1)
            limit = local[m, :]
            mine[m, :] = jnp.sum(
                jnp.where(ladder <= limit, first, 0.0) + jnp.where(ladder < limit, second, 0.0),
                axis=0,
                keepdims=True,
            )
        return carry

    lax.fori_loop(0, slots // UNROLL, reach, 0)
    part_copies = [
        pltpu.make_async_remote_copy(
            src_ref=mine, dst_ref=parts.at[k - 1], send_sem=part_send.at[k - 1],
            recv_sem=part_recv.at[k - 1], device_id=peer(k), device_id_type=MESH,
        )
        for k in range(1, n_rad)
    ]
    for copy in part_copies:
        copy.start()
    for copy in part_copies:
        copy.wait_recv()
    pred = mine[...]
    for k in range(1, n_rad):
        pred = pred + parts[k - 1]
    res = jnp.where(live, (step_len * pred - observed) * inverse, 0.0)
    terms[...] = res * inverse

    def collected(step, sums):
        first, second = sums
        for n in range(UNROLL):
            m = pl.ds(step * UNROLL + n, 1)
            limit, term = local[m, :], terms[m, :]
            first = first + jnp.where(ladder <= limit, term, 0.0)
            second = second + jnp.where(ladder < limit, term, 0.0)
        return first, second

    nothing = jnp.zeros((depth, pixels), f32)
    first, second = lax.fori_loop(0, slots // UNROLL, collected, (nothing, nothing))
    first, second = first.T, second.T
    for q in range(8):
        suffix = (first, second)[q % 2][(q // 2) * cols : (q // 2 + 1) * cols]
        slopes[q, PAD : PAD + cols] = dens[q] * step_len * suffix

    def collect(u):
        def child(q, sums):
            sums = list(sums)
            for v in range(3):
                window = slopes[q, PAD + 1 - v : PAD + 1 - v + cols, :]
                for w in range(3):
                    sums[w] = sums[w] + weights[9 * u + 3 * v + w, pl.ds(q, 1), :] * window
            return tuple(sums)

        sums = lax.fori_loop(0, 8, child, tuple(jnp.zeros((cols, depth), f32) for _ in range(3)))
        back_edges_out[0, u] = pack(sums[0][:, 0:1])
        back_edges_out[1, u] = pack(sums[2][:, depth - 1 : depth])
        low = jnp.where(lane == depth - 1, 0.0, pltpu.roll(sums[0], depth - 1, 1))
        high = jnp.where(lane == 0, 0.0, pltpu.roll(sums[2], 1, 1))
        return sums[1] + low + high

    own = None
    for u in (0, 2, 1):
        result = collect(u)
        if u == 1:
            own = result
        else:
            back_rows_out[u // 2] = result
        for n, (du, dz) in enumerate(AROUND):
            if du == u - 1:
                pl.when(exists(du, dz))(back_copies[n].start)

    def unmix(q, grads):
        slope = slopes[q, PAD : PAD + cols, :]
        return tuple(grads[p] + mixing[q, p : p + 1, :] * slope for p in range(8))

    grads = lax.fori_loop(0, 8, unmix, tuple(blocks[p] for p in range(8)))
    for p in range(8):
        dens[p] = grads[p]
    even_lane = lane % 2 == 0

    def join(i, carry):
        for j in range(2):
            even, odd = dens[4 * i + 2 * j], dens[4 * i + 2 * j + 1]
            for side in range(2):
                index = side * half + lane // 2
                out_excite[side, i, pl.ds(j, cols, stride=2), :] = jnp.where(
                    even_lane, picked(even, index), picked(odd, index)
                )
        return carry

    lax.fori_loop(0, 2, join, 0)

    for n, (du, dz) in enumerate(AROUND):
        pl.when(exists(-du, -dz))(back_copies[n].wait_recv)
    near = unpack(back_edges[0, 0] + back_edges[0, 1] + back_edges[0, 2])
    far = unpack(back_edges[1, 0] + back_edges[1, 1] + back_edges[1, 2])
    own = own + back_rows[0] + back_rows[1]
    own = own + jnp.where(lane == 0, near, 0.0) + jnp.where(lane == depth - 1, far, 0.0)
    out_coarse[...] = own
    for n, (du, dz) in enumerate(AROUND):
        pl.when(exists(du, dz))(halo_copies[n].wait_send)
        pl.when(exists(du, dz))(back_copies[n].wait_send)
    for copy in part_copies:
        copy.wait_send()


def write(halves, block, grad_excite, grad_coarse, sem):
    depth = block.shape[1]
    pairs = [(halves.at[side], grad_excite.at[:, :, pl.ds(side * depth, depth)]) for side in range(2)]
    pairs.append((block, grad_coarse))
    copies = [
        pltpu.make_async_copy(source, target, sem.at[n])
        for n, (source, target) in enumerate(pairs)
    ]
    for copy in copies:
        copy.start()
    for copy in copies:
        copy.wait()


def per_device(coarse, excite, kernels, mixing, star_bin, star_count, star_obs, star_isig):
    samples, rows, cols, depth = coarse.shape
    slots = star_bin.shape[2]
    n_ang, n_rad = lax.axis_size("ang"), lax.axis_size("rad")
    assert slots % UNROLL == 0 and samples == 1 and rows == 1 and 4 * cols == depth
    f32 = jnp.float32
    vmem, dma = pltpu.VMEM, pltpu.SemaphoreType.DMA
    anywhere = pl.BlockSpec(memory_space=pl.ANY)
    padded = cols + 2 * PAD
    swap = lambda stars: jnp.swapaxes(stars, 1, 2)
    results = pl.pallas_call(
        functools.partial(kernel, n_ang, n_rad),
        out_shape=[vmem((2, 2, 2 * cols, depth), f32), vmem((cols, depth), f32)],
        in_specs=[pl.BlockSpec(memory_space=pltpu.HBM)] * 8,
        out_specs=[pl.BlockSpec(memory_space=vmem)] * 2,
        scratch_shapes=[
            vmem((cols, depth), f32),
            vmem((2, 2, 2 * cols, depth), f32),
            vmem((27, 8, depth), f32),
            vmem((8, 8, depth), f32),
            vmem((2, slots, 2 * cols), jnp.int32),
            vmem((2, 2 * cols), jnp.int32),
            vmem((2, slots, 2 * cols), f32),
            vmem((2, slots, 2 * cols), f32),
            vmem((2, 1, depth), f32),
            vmem((2, cols, depth), f32),
            vmem((2, 3, 1, depth), f32),
            vmem((3, 3, padded, depth), f32),
            vmem((8, cols, depth), f32),
            vmem((8, cols, depth), f32),
            vmem((slots, depth), f32),
            vmem((n_rad - 1, slots, depth), f32),
            vmem((slots, depth), jnp.int32),
            vmem((slots, depth), f32),
            vmem((8, padded, depth), f32),
            vmem((2, cols, depth), f32),
            vmem((2, 3, 1, depth), f32),
            vmem((2, cols, depth), f32),
            vmem((2, 3, 1, depth), f32),
            dma((9,)),
            dma((8,)),
            dma((8,)),
            dma((n_rad - 1,)),
            dma((n_rad - 1,)),
            dma((8,)),
            dma((8,)),
        ],
        compiler_params=pltpu.CompilerParams(
            collective_id=0, has_side_effects=True, vmem_limit_bytes=8 << 20
        ),
    )(
        *(
            pltpu.with_memory_space_constraint(argument, pltpu.HBM)
            for argument in (
                coarse[0, 0],
                excite[0],
                kernels,
                mixing,
                swap(star_bin),
                star_count,
                swap(star_obs),
                swap(star_isig),
            )
        )
    )
    grad_excite, grad_coarse = pl.pallas_call(
        write,
        out_shape=[
            jax.ShapeDtypeStruct(excite.shape[1:], f32),
            jax.ShapeDtypeStruct((cols, depth), f32),
        ],
        in_specs=[anywhere] * 2,
        out_specs=[pl.BlockSpec(memory_space=pltpu.HBM)] * 2,
        scratch_shapes=[dma((3,))],
        compiler_params=pltpu.CompilerParams(vmem_limit_bytes=1 << 20),
    )(*results)
    return grad_excite[None], grad_coarse[None, None]


def solution(mesh):
    in_specs = (
        P(None, "ang", None, "rad"),
        P(None, "ang", None, "rad"),
        P(),
        P(),
        P("ang", None, None),
        P("ang", None),
        P("ang", None, None),
        P("ang", None, None),
    )
    out_specs = (P(None, "ang", None, "rad"), P(None, "ang", None, "rad"))
    return jax.shard_map(
        per_device, mesh=mesh, in_specs=in_specs, out_specs=out_specs, check_vma=False
    )
```

```python
import functools

import jax
import jax.numpy as jnp
from jax import lax
from jax.experimental import pallas as pl
from jax.experimental.pallas import tpu as pltpu
from jax.sharding import PartitionSpec as P

MESH = pl.DeviceIdType.MESH
AROUND = [(du, dz) for du in (-1, 0, 1) for dz in (-1, 0, 1) if (du, dz) != (0, 0)]
AROUND.sort(key=lambda step: -abs(step[0]) - abs(step[1]))
PAD = 8
SHARES = 2


def kernel(
    n_ang,
    n_rad,
    coarse_hbm,
    excite_hbm,
    weights_hbm,
    mixing_hbm,
    bin_hbm,
    count_hbm,
    obs_hbm,
    isig_hbm,
    out_excite,
    out_coarse,
    coarse,
    excite,
    weights,
    mixing,
    bins,
    count,
    obs,
    isig,
    edge_out,
    halo_rows,
    halo_edges,
    windows,
    blocks,
    dens,
    mine,
    parts,
    slopes,
    back_rows_out,
    back_edges_out,
    back_rows,
    back_edges,
    load_sem,
    halo_send,
    halo_recv,
    part_send,
    part_recv,
    back_send,
    back_recv,
):
    ang = lax.axis_index("ang")
    rad = lax.axis_index("rad")
    cols, depth = coarse.shape
    slots = mine.shape[0]
    half = depth // 2
    step_len = 1.0 / (2 * depth * n_rad)
    f32 = jnp.float32

    def exists(du, dz):
        there = None
        for shift, place, size in ((du, ang, n_ang), (dz, rad, n_rad)):
            if shift == 0:
                continue
            ok = place > 0 if shift < 0 else place < size - 1
            there = ok if there is None else jnp.logical_and(there, ok)
        return there

    def at(du, dz):
        return {"ang": ang + du, "rad": rad + dz}

    def peer(k):
        return {"ang": ang, "rad": lax.rem(rad + k, n_rad)}

    here = pl.ds(pl.multiple_of(rad * depth, depth), depth)
    pairs = [
        (coarse_hbm, coarse),
        (excite_hbm.at[:, :, pl.ds(0, depth)], excite.at[0]),
        (excite_hbm.at[:, :, pl.ds(depth, depth)], excite.at[1]),
        (mixing_hbm.at[:, :, here], mixing),
        (weights_hbm.at[:, :, here], weights),
        (bin_hbm, bins),
        (count_hbm, count),
        (obs_hbm, obs),
        (isig_hbm, isig),
    ]
    loads = [
        pltpu.make_async_copy(source, target, load_sem.at[n])
        for n, (source, target) in enumerate(pairs)
    ]
    loads[0].start()

    barrier = pltpu.get_barrier_semaphore()
    beside = [(du, dz) for du, dz in AROUND if du != 0]
    for du, dz in beside:

        @pl.when(exists(du, dz))
        def _():
            pl.semaphore_signal(barrier, inc=1, device_id=at(du, dz), device_id_type=MESH)

    for k in range(1, n_rad):
        pl.semaphore_signal(barrier, inc=1, device_id=peer(k), device_id_type=MESH)
    for load in loads[1:]:
        load.start()

    rows_of = lambda du: 0 if du < 0 else 1
    halo_copies, back_copies, targets = [], [], []
    for n, (du, dz) in enumerate(AROUND):
        if dz == 0:
            source, target = coarse, halo_rows.at[rows_of(-du)]
            back_source, back_target = back_rows_out.at[rows_of(du)], back_rows.at[rows_of(-du)]
        else:
            source, target = edge_out.at[rows_of(dz)], halo_edges.at[rows_of(-dz), 1 - du]
            back_source = back_edges_out.at[rows_of(dz), 1 + du]
            back_target = back_edges.at[rows_of(-dz), 1 - du]
        halo_copies.append(
            pltpu.make_async_remote_copy(
                src_ref=source, dst_ref=target, send_sem=halo_send.at[n],
                recv_sem=halo_recv.at[n], device_id=at(du, dz), device_id_type=MESH,
            )
        )
        back_copies.append(
            pltpu.make_async_remote_copy(
                src_ref=back_source, dst_ref=back_target, send_sem=back_send.at[n],
                recv_sem=back_recv.at[n], device_id=at(du, dz), device_id_type=MESH,
            )
        )
        targets.append((target, back_target))

    lane = lax.broadcasted_iota(jnp.int32, (cols, depth), 1)
    row = lax.broadcasted_iota(jnp.int32, (cols, depth), 0)
    diagonal = lane == row

    def pack(column):
        return jnp.sum(jnp.where(diagonal, column, 0.0), axis=0, keepdims=True)

    def unpack(packed):
        return jnp.sum(jnp.where(diagonal, packed, 0.0), axis=1, keepdims=True)

    loads[0].wait()
    middle = coarse[...]
    edge_out[0] = pack(middle[:, 0:1])
    edge_out[1] = pack(middle[:, depth - 1 : depth])

    sides = [jnp.where(place > 0, 1, 0) + jnp.where(place < size - 1, 1, 0)
             for place, size in ((ang, n_ang), (rad, n_rad))]
    pl.semaphore_wait(barrier, sides[0] * (sides[1] + 1) + n_rad - 1)
    for n, (du, dz) in enumerate(AROUND):
        pl.when(exists(du, dz))(halo_copies[n].start)

    for (du, dz), (target, back_target) in zip(AROUND, targets):

        @pl.when(jnp.logical_not(exists(-du, -dz)))
        def _():
            target[...] = jnp.zeros(target.shape, f32)
            back_target[...] = jnp.zeros(back_target.shape, f32)

    for load in loads[1:]:
        load.wait()

    place = lax.broadcasted_iota(jnp.int32, (slots, depth), 1)
    slot = lax.broadcasted_iota(jnp.int32, (slots, depth), 0)
    group, member = place // cols, place % cols
    order = (group // 2) * (2 * cols) + 2 * member + group % 2

    def wide(ref):
        return jnp.concatenate([ref[0], ref[1]], axis=1)

    def picked(values, index):
        return jnp.take_along_axis(values, index, axis=1, mode="promise_in_bounds")

    counts = jnp.concatenate([count[0:1], count[1:2]], axis=1)
    inverse = picked(jnp.where(slot < counts, wide(isig), 0.0), order)
    live = inverse > 0.0
    observed = picked(wide(obs), order)
    local = picked(wide(bins), order) - rad * (2 * depth)

    evens = (2 * lane) % depth + lane // half
    odds = (2 * lane + 1) % depth - lane // half
    children = [None] * 8
    for i in range(2):
        for j in range(2):
            low = picked(excite[0, i, pl.ds(j, cols, stride=2), :], evens)
            high = picked(excite[1, i, pl.ds(j, cols, stride=2), :], odds)
            q = 4 * i + 2 * j
            children[q] = jnp.where(lane < half, low, high)
            children[q + 1] = pltpu.roll(jnp.where(lane < half, high, low), half, 1)
            blocks[q] = children[q]
            blocks[q + 1] = children[q + 1]
    fine = []
    for q in range(8):
        total = mixing[q, 0:1, :] * children[0]
        for p in range(1, 8):
            total = total + mixing[q, p : p + 1, :] * children[p]
        fine.append(total)

    blank = jnp.zeros((PAD, depth), f32)
    for u in range(3):
        for w in range(3):
            windows[u, w, 0:PAD] = blank
            windows[u, w, PAD + cols : 2 * PAD + cols] = blank
    for q in range(8):
        slopes[q, 0:PAD] = blank
        slopes[q, PAD + cols : 2 * PAD + cols] = blank

    def gather(u, base):
        near, far = unpack(halo_edges[0, u]), unpack(halo_edges[1, u])
        inner = pl.ds(PAD, cols)
        windows[u, 0, inner] = jnp.where(lane == 0, near, pltpu.roll(base, 1, 1))
        windows[u, 2, inner] = jnp.where(lane == depth - 1, far, pltpu.roll(base, depth - 1, 1))

    def spread(u, ws, fine):
        for v in range(3):
            for w in ws:
                window = windows[u, w, PAD - 1 + v : PAD - 1 + v + cols, :]
                t = 9 * u + 3 * v + w
                fine = [
                    fine[q] + weights[t, q : q + 1, :] * window for q in range(8)
                ]
        return fine

    windows[1, 1, PAD : PAD + cols] = middle
    fine = spread(1, (1,), fine)
    def arrived(choose):
        for n, (du, dz) in enumerate(AROUND):
            if choose(du, dz):
                pl.when(exists(-du, -dz))(halo_copies[n].wait_recv)

    arrived(lambda du, dz: du == 0)
    gather(1, middle)
    fine = spread(1, (0, 2), fine)
    arrived(lambda du, dz: dz == 0)
    for u in (0, 2):
        windows[u, 1, PAD : PAD + cols] = halo_rows[u // 2]
        fine = spread(u, (1,), fine)
    arrived(lambda du, dz: du != 0 and dz != 0)
    for u in (0, 2):
        gather(u, halo_rows[u // 2])
        fine = spread(u, (0, 2), fine)
    for q in range(8):
        dens[q] = jnp.exp(fine[q])

    pixels = 4 * cols
    ladder = 2 * lax.broadcasted_iota(jnp.int32, (depth, pixels), 0)
    first = jnp.concatenate([dens[q] for q in range(0, 8, 2)], axis=0).T
    second = jnp.concatenate([dens[q] for q in range(1, 8, 2)], axis=0).T
    share = slots // SHARES
    part_copies = []
    for group in range(SHARES):
        for m in range(group * share, (group + 1) * share):
            limit = local[m : m + 1, :]
            mine[m : m + 1, :] = jnp.sum(
                jnp.where(ladder <= limit, first, 0.0) + jnp.where(ladder < limit, second, 0.0),
                axis=0,
                keepdims=True,
            )
        slab = pl.ds(group * share, share)
        for k in range(1, n_rad):
            part_copies.append(
                pltpu.make_async_remote_copy(
                    src_ref=mine.at[slab], dst_ref=parts.at[k - 1, slab],
                    send_sem=part_send.at[group, k - 1], recv_sem=part_recv.at[group, k - 1],
                    device_id=peer(k), device_id_type=MESH,
                )
            )
            part_copies[-1].start()

    first = jnp.zeros((depth, pixels), f32)
    second = jnp.zeros((depth, pixels), f32)
    for group in range(SHARES):
        slab = slice(group * share, (group + 1) * share)
        for copy in part_copies[group * (n_rad - 1) : (group + 1) * (n_rad - 1)]:
            copy.wait_recv()
        pred = mine[slab]
        for k in range(1, n_rad):
            pred = pred + parts[k - 1, slab]
        weight = inverse[slab]
        res = jnp.where(live[slab], (step_len * pred - observed[slab]) * weight, 0.0)
        terms = res * weight * step_len
        for m in range(share):
            limit = local[group * share + m : group * share + m + 1, :]
            term = terms[m : m + 1, :]
            first = first + jnp.where(ladder <= limit, term, 0.0)
            second = second + jnp.where(ladder < limit, term, 0.0)
    first, second = first.T, second.T
    for q in range(8):
        suffix = (first, second)[q % 2][(q // 2) * cols : (q // 2 + 1) * cols]
        slopes[q, PAD : PAD + cols] = dens[q] * suffix

    def collect(u):
        sums = [None] * 3
        for v in range(3):
            for q in range(8):
                window = slopes[q, PAD + 1 - v : PAD + 1 - v + cols, :]
                for w in range(3):
                    term = weights[9 * u + 3 * v + w, q : q + 1, :] * window
                    sums[w] = term if sums[w] is None else sums[w] + term
        back_edges_out[0, u] = pack(sums[0][:, 0:1])
        back_edges_out[1, u] = pack(sums[2][:, depth - 1 : depth])
        low = jnp.where(lane == depth - 1, 0.0, pltpu.roll(sums[0], depth - 1, 1))
        high = jnp.where(lane == 0, 0.0, pltpu.roll(sums[2], 1, 1))
        return sums[1] + low + high

    own = None
    for u in (0, 2, 1):
        result = collect(u)
        if u == 1:
            own = result
        else:
            back_rows_out[u // 2] = result
        for n, (du, dz) in enumerate(AROUND):
            if du == u - 1:
                pl.when(exists(du, dz))(back_copies[n].start)

    grads = []
    for p in range(8):
        total = blocks[p]
        for q in range(8):
            total = total + mixing[q, p : p + 1, :] * slopes[q, PAD : PAD + cols, :]
        grads.append(total)
    even_lane = lane % 2 == 0
    for i in range(2):
        for j in range(2):
            q = 4 * i + 2 * j
            for side in range(2):
                index = side * half + lane // 2
                out_excite[side, i, pl.ds(j, cols, stride=2), :] = jnp.where(
                    even_lane, picked(grads[q], index), picked(grads[q + 1], index)
                )
    for n, (du, dz) in enumerate(AROUND):
        pl.when(exists(-du, -dz))(back_copies[n].wait_recv)
    near = unpack(back_edges[0, 0] + back_edges[0, 1] + back_edges[0, 2])
    far = unpack(back_edges[1, 0] + back_edges[1, 1] + back_edges[1, 2])
    own = own + back_rows[0] + back_rows[1]
    own = own + jnp.where(lane == 0, near, 0.0) + jnp.where(lane == depth - 1, far, 0.0)
    out_coarse[...] = own
    for n, (du, dz) in enumerate(AROUND):
        pl.when(exists(du, dz))(halo_copies[n].wait_send)
        pl.when(exists(du, dz))(back_copies[n].wait_send)
    for copy in part_copies:
        copy.wait_send()


def write(halves, block, grad_excite, grad_coarse, sem):
    depth = block.shape[1]
    pairs = [(halves.at[side], grad_excite.at[:, :, pl.ds(side * depth, depth)]) for side in range(2)]
    pairs.append((block, grad_coarse))
    copies = [
        pltpu.make_async_copy(source, target, sem.at[n])
        for n, (source, target) in enumerate(pairs)
    ]
    for copy in copies:
        copy.start()
    for copy in copies:
        copy.wait()


def per_device(coarse, excite, kernels, mixing, star_bin, star_count, star_obs, star_isig):
    samples, rows, cols, depth = coarse.shape
    slots = star_bin.shape[2]
    n_ang, n_rad = lax.axis_size("ang"), lax.axis_size("rad")
    assert samples == 1 and rows == 1 and 4 * cols == depth
    f32 = jnp.float32
    vmem, dma = pltpu.VMEM, pltpu.SemaphoreType.DMA
    anywhere = pl.BlockSpec(memory_space=pl.ANY)
    padded = cols + 2 * PAD
    swap = lambda stars: jnp.swapaxes(stars, 1, 2)
    results = pl.pallas_call(
        functools.partial(kernel, n_ang, n_rad),
        out_shape=[vmem((2, 2, 2 * cols, depth), f32), vmem((cols, depth), f32)],
        in_specs=[pl.BlockSpec(memory_space=pltpu.HBM)] * 8,
        out_specs=[pl.BlockSpec(memory_space=vmem)] * 2,
        scratch_shapes=[
            vmem((cols, depth), f32),
            vmem((2, 2, 2 * cols, depth), f32),
            vmem((27, 8, depth), f32),
            vmem((8, 8, depth), f32),
            vmem((2, slots, 2 * cols), jnp.int32),
            vmem((2, 2 * cols), jnp.int32),
            vmem((2, slots, 2 * cols), f32),
            vmem((2, slots, 2 * cols), f32),
            vmem((2, 1, depth), f32),
            vmem((2, cols, depth), f32),
            vmem((2, 3, 1, depth), f32),
            vmem((3, 3, padded, depth), f32),
            vmem((8, cols, depth), f32),
            vmem((8, cols, depth), f32),
            vmem((slots, depth), f32),
            vmem((n_rad - 1, slots, depth), f32),
            vmem((8, padded, depth), f32),
            vmem((2, cols, depth), f32),
            vmem((2, 3, 1, depth), f32),
            vmem((2, cols, depth), f32),
            vmem((2, 3, 1, depth), f32),
            dma((9,)),
            dma((8,)),
            dma((8,)),
            dma((SHARES, n_rad - 1)),
            dma((SHARES, n_rad - 1)),
            dma((8,)),
            dma((8,)),
        ],
        compiler_params=pltpu.CompilerParams(
            collective_id=0, has_side_effects=True, vmem_limit_bytes=8 << 20
        ),
    )(
        *(
            pltpu.with_memory_space_constraint(argument, pltpu.HBM)
            for argument in (
                coarse[0, 0],
                excite[0],
                kernels,
                mixing,
                swap(star_bin),
                star_count,
                swap(star_obs),
                swap(star_isig),
            )
        )
    )
    grad_excite, grad_coarse = pl.pallas_call(
        write,
        out_shape=[
            jax.ShapeDtypeStruct(excite.shape[1:], f32),
            jax.ShapeDtypeStruct((cols, depth), f32),
        ],
        in_specs=[anywhere] * 2,
        out_specs=[pl.BlockSpec(memory_space=pltpu.HBM)] * 2,
        scratch_shapes=[dma((3,))],
        compiler_params=pltpu.CompilerParams(vmem_limit_bytes=1 << 20),
    )(*results)
    return grad_excite[None], grad_coarse[None, None]


def solution(mesh):
    in_specs = (
        P(None, "ang", None, "rad"),
        P(None, "ang", None, "rad"),
        P(),
        P(),
        P("ang", None, None),
        P("ang", None),
        P("ang", None, None),
        P("ang", None, None),
    )
    out_specs = (P(None, "ang", None, "rad"), P(None, "ang", None, "rad"))
    return jax.shard_map(
        per_device, mesh=mesh, in_specs=in_specs, out_specs=out_specs, check_vma=False
    )
```
